32 devices in a mesh: group: 2 (over x), wide: 8 (over z, y), narrow: 2 (over core).
Axes of the slice: x: 2, y: 2, z: 4, core: 2. Of those that a mesh axis runs over, the one named last changes fastest.
Arguments:
- embeds: bfloat16 [4, 64, 5120], P(None, ('group', 'wide'), 'narrow'), parts along dimension 1, may hold values from -120 to 120
- lengths: int32 [64], P(('group', 'wide')), parts along dimension 0, may hold values from 1 to 384, 6144 in all
- k_cache: bfloat16 [64, 8, 384, 128], P(('group', 'wide'), 'narrow'), parts along dimension 0, may hold values from -175 to 175
- v_cache: bfloat16 [64, 8, 384, 128], P(('group', 'wide'), 'narrow'), parts along dimension 0, may hold values from -4 to 4
- gain_attn: bfloat16 [5120], P('narrow'), may hold values from 0.25 to 1.75
- gain_ffn: bfloat16 [5120], P('narrow'), may hold values from 0.25 to 1.75
- w_query: bfloat16 [5120, 5120], P('narrow', 'wide'), may hold values from -0.078125 to 0.078125
- w_key: bfloat16 [5120, 1024], P('narrow', 'wide'), may hold values from -0.078125 to 0.078125
- w_value: bfloat16 [5120, 1024], P('narrow', 'wide'), may hold values from -0.078125 to 0.078125
- w_out: bfloat16 [5120, 5120], P('narrow', 'wide'), may hold values from -0.078125 to 0.078125
- w_gate: bfloat16 [5120, 14336], P('narrow', 'wide'), may hold values from -0.078125 to 0.078125
- w_up: bfloat16 [5120, 14336], P('narrow', 'wide'), may hold values from -0.078125 to 0.078125
- w_down: bfloat16 [14336, 5120], P('wide', 'narrow'), may hold values from -0.046875 to 0.046875
Outputs:
- hidden_out: float32 [4, 64, 5120], P(None, ('group', 'wide'), 'narrow'), parts along dimension 1
- new_keys: bfloat16 [64, 8, 4, 128], P(('group', 'wide'), 'narrow'), parts along dimension 0
- new_values: bfloat16 [64, 8, 4, 128], P(('group', 'wide'), 'narrow'), parts along dimension 0
The draws below stay inside these ranges and needn't reach their ends.
There are 2 independent parts, one for each index of `group`. The reference program is written for one: setup_inputs(seed, part) draws one part's arguments, and reference() takes and returns one part's arrays. A program takes and returns all parts, laid end to end along the dimension named above; an argument that names none is the same for every part. Nothing has to cross between parts.
Inputs may be any that keep to these rules, and one draw needn't show every extreme that they name: In every part one rollout has all 384 cache positions valid, and the lengths of the 32 rollouts of one part sum to 6144.
All inputs are finite; a program needn't handle non-finite values. No bound on the sum of `lengths` on one device may be relied on, other than what follows from the above.
Results may differ from the reference program's by a relative error of at most 0.0051.
Values may be sent and summed in bfloat16 or wider, within the bound.
A program may use at most 128 MiB of HBM per device.

```python
import math
import jax
import jax.numpy as jnp
import numpy as np
from jax import lax

D = 5120
HQ = 40
KVH = 8
HD = 128
FF = 14336
STEPS = 4
CTX = 384
ROLL = 32


def shaped_draw(base_part, row_key, column_key, row_spread, slope):
    place_along = jnp.arange(D, dtype=jnp.float32) / D - 0.5
    row_scale = jnp.exp(jax.random.uniform(row_key, (STEPS, ROLL, 1), jnp.float32, -row_spread, row_spread))
    column_scale = jnp.exp(jax.random.uniform(column_key, (D,), jnp.float32, -1.15, 1.15) + slope * place_along)
    return (base_part * row_scale * column_scale).astype(jnp.bfloat16)


def draw_embeds(key, part):
    key = jax.random.fold_in(key, 11)
    base_key, row_key, column_key = jax.random.split(key, 3)
    base_part = jnp.clip(jax.random.normal(base_key, (STEPS, ROLL, D), jnp.float32), -4.0, 4.0)
    return shaped_draw(base_part, row_key, column_key, 1.15, 1.1)


def draw_k_cache(key, part):
    key = jax.random.fold_in(key, 23)
    base_key = jax.random.fold_in(key, 0)
    base_part = jnp.clip(jax.random.normal(base_key, (ROLL, KVH, CTX, HD), jnp.float32), -4.0, 4.0)
    return base_part.astype(jnp.bfloat16)


def block_levels(stream_key, shape, shards, least, high):
    factor_of = 1.0
    for axis_at, shards_of in shards:
        heights = jax.random.uniform(jax.random.fold_in(jax.random.fold_in(stream_key, 6), axis_at), (shards_of,), jnp.float32, least / len(shards), high / len(shards))
        factor_of = factor_of * jnp.repeat(jnp.exp(heights), shape[axis_at] // shards_of).reshape((-1,) + (1,) * (len(shape) - 1 - axis_at))
    return factor_of


def split_up(count, total, limit, skew):
    weights = [(1 << 20) // math.isqrt(grade ** skew) + 1 for grade in range(2, count + 1)]
    rest, given = total - limit - (count - 1), [1] * (count - 1)
    while rest > 0:
        candidates = [i for i in range(count - 1) if given[i] < limit]
        pool, remaining = sum([weights[i] for i in candidates]), rest
        for i in candidates:
            more = min(limit - given[i], max(1, remaining * weights[i] // pool), rest)
            given[i] = given[i] + more
            rest = rest - more
    return np.array([limit] + given)


def uneven(own_key, number_of, total, bound, lean):
    if number_of == 2:
        one = jax.random.randint(own_key, (), max(1, total - bound), min(bound, total - 1) + 1)
        return jnp.stack([one, total - one])
    sizes = jnp.asarray(split_up(number_of, total, bound, lean), jnp.int32)
    couples = (number_of - 1) // 2
    source_of, sink = sizes[1:1 + 2 * couples:2], sizes[2:2 + 2 * couples:2]
    room = jnp.minimum(source_of - 1, bound - sink)
    shifted = jax.random.randint(jax.random.fold_in(own_key, 1), (couples,), 0, 1 << 20) % (room + 1)
    sizes = sizes.at[1:1 + 2 * couples:2].set(source_of - shifted).at[2:2 + 2 * couples:2].set(sink + shifted)
    return sizes[jax.random.permutation(jax.random.fold_in(own_key, 2), number_of)]


def normal_values(rng, dims, width, bound, pieces=(), held_as=jnp.bfloat16):
    result = jax.random.normal(rng, dims, jnp.float32) * width
    if len(pieces) > 0:
        result = block_levels(rng, dims, pieces, -0.22, 0.18) * result
    return jnp.clip(result, min=-bound, max=bound).astype(held_as)


def setup_inputs(seed: int = 0, part: int = 0) -> dict:
    streams_of = jax.random.split(jax.random.key(seed), 14)
    own_keys = jax.random.split(jax.random.fold_in(streams_of[13], part), 14)
    return {
        "embeds": draw_embeds(jax.random.fold_in(jax.random.fold_in(streams_of[13], part), 71), part),
        "lengths": uneven(own_keys[1], ROLL, ROLL * CTX // 2, CTX, 2).astype(jnp.int32),
        "k_cache": draw_k_cache(jax.random.fold_in(jax.random.fold_in(streams_of[13], part), 71), part),
        "v_cache": normal_values(own_keys[3], (ROLL, KVH, CTX, HD), 1.0, 4.0, ((0, 8), (1, 2))),
        "gain_attn": jnp.clip(1.0 + 0.15 * jax.random.normal(streams_of[4], (D,), jnp.float32), 0.25, 1.75).astype(jnp.bfloat16),
        "gain_ffn": jnp.clip(1.0 + 0.15 * jax.random.normal(streams_of[5], (D,), jnp.float32), 0.25, 1.75).astype(jnp.bfloat16),
        "w_query": normal_values(streams_of[6], (D, HQ * HD), D ** -0.5, 0.078125, ((0, 2), (1, 8))),
        "w_key": normal_values(streams_of[7], (D, KVH * HD), D ** -0.5, 0.078125, ((0, 2), (1, 8))),
        "w_value": normal_values(streams_of[8], (D, KVH * HD), D ** -0.5, 0.078125, ((0, 2), (1, 8))),
        "w_out": normal_values(streams_of[9], (HQ * HD, D), (HQ * HD) ** -0.5, 0.078125, ((0, 2), (1, 8))),
        "w_gate": normal_values(streams_of[10], (D, FF), D ** -0.5, 0.078125, ((0, 2), (1, 8))),
        "w_up": normal_values(streams_of[11], (D, FF), D ** -0.5, 0.078125, ((0, 2), (1, 8))),
        "w_down": normal_values(streams_of[12], (FF, D), FF ** -0.5, 0.046875, ((0, 8), (1, 2))),
    }


rope_base = 1000000.0
norm_eps = 1e-06

def angles_for(positions, head_dim):
    steps_up = jnp.arange(head_dim // 2, dtype=jnp.float32)
    inverse = jnp.exp(steps_up * (-2.0 * math.log(rope_base) / head_dim))
    return positions.astype(jnp.float32)[..., None] * inverse

def rotate(values, angles):
    half_dim = values.shape[-1] // 2
    cosine = jnp.cos(angles)
    sine_part = jnp.sin(angles)
    leading = values[..., :half_dim]
    trailing = values[..., half_dim:]
    return jnp.concatenate([leading * cosine - trailing * sine_part, trailing * cosine + leading * sine_part], axis=-1)

def normalize(tokens, gain_row):
    mean_square = lax.optimization_barrier(jnp.mean(tokens * tokens, axis=-1, keepdims=True))
    return (tokens * lax.rsqrt(mean_square + norm_eps) * gain_row.astype(jnp.float32)).astype(jnp.bfloat16)

def reference(embeds, lengths, k_cache, v_cache, gain_attn, gain_ffn, w_query, w_key, w_value, w_out, w_gate, w_up, w_down):
    group_size = HQ // KVH
    score_scale = 1.0 / math.sqrt(HD)
    cache_live = jnp.arange(CTX, dtype=jnp.int32)[None, :] < lengths[:, None]
    cache_keys = k_cache.astype(jnp.float32)
    cache_values = v_cache.astype(jnp.float32)
    fresh_keys = []
    fresh_values = []
    outputs = []
    for step_index in range(STEPS):
        tokens = embeds[step_index].astype(jnp.float32)
        normed = normalize(tokens, gain_attn)
        queries = jnp.dot(normed, w_query, preferred_element_type=jnp.float32).reshape(ROLL, HQ, HD)
        keys_now = jnp.dot(normed, w_key, preferred_element_type=jnp.float32).reshape(ROLL, KVH, HD)
        values_now = jnp.dot(normed, w_value, preferred_element_type=jnp.float32).reshape(ROLL, KVH, HD).astype(jnp.bfloat16)
        angles = angles_for(lengths + step_index, HD)[:, None, :]
        queries = rotate(queries, angles).astype(jnp.bfloat16)
        keys_now = rotate(keys_now, angles).astype(jnp.bfloat16)
        fresh_keys.append(keys_now)
        fresh_values.append(values_now)
        stacked_keys = lax.optimization_barrier(jnp.stack(fresh_keys, axis=2)).astype(jnp.float32)
        stacked_values = lax.optimization_barrier(jnp.stack(fresh_values, axis=2)).astype(jnp.float32)
        grouped = lax.optimization_barrier(queries).reshape(ROLL, KVH, group_size, HD).astype(jnp.float32)
        old_scores = jnp.einsum('rkgd,rkcd->rkgc', grouped, cache_keys) * score_scale
        old_scores = jnp.where(cache_live[:, None, None, :], old_scores, -jnp.inf)
        new_scores = jnp.einsum('rkgd,rktd->rkgt', grouped, stacked_keys) * score_scale
        scores = jnp.concatenate([old_scores, new_scores], axis=-1)
        largest = lax.optimization_barrier(jnp.max(scores, axis=-1, keepdims=True))
        weights = jnp.exp(scores - largest)
        probabilities = (weights / lax.optimization_barrier(jnp.sum(weights, axis=-1, keepdims=True))).astype(jnp.bfloat16)
        probabilities = lax.optimization_barrier(probabilities).astype(jnp.float32)
        mixed_heads = jnp.einsum('rkgc,rkcd->rkgd', probabilities[..., :CTX], cache_values)
        mixed_heads = mixed_heads + jnp.einsum('rkgt,rktd->rkgd', probabilities[..., CTX:], stacked_values)
        mixed_heads = mixed_heads.reshape(ROLL, HQ * HD).astype(jnp.bfloat16)
        residual = tokens + jnp.dot(mixed_heads, w_out, preferred_element_type=jnp.float32)
        normed_ffn = normalize(residual, gain_ffn)
        gate_value = jnp.dot(normed_ffn, w_gate, preferred_element_type=jnp.float32)
        upward = jnp.dot(normed_ffn, w_up, preferred_element_type=jnp.float32)
        hidden = (jax.nn.silu(gate_value) * upward).astype(jnp.bfloat16)
        outputs.append(residual + jnp.dot(hidden, w_down, preferred_element_type=jnp.float32))
    return (jnp.stack(outputs), jnp.stack(fresh_keys, axis=2), jnp.stack(fresh_values, axis=2))
```

```python
import math

import jax
import jax.numpy as jnp
from jax import lax
from jax.sharding import PartitionSpec as P

HQ = 40
KVH = 8
HD = 128
STEPS = 4


rope_base = 1000000.0
norm_eps = 1e-06


def angles_for(positions, head_dim):
    steps_up = jnp.arange(head_dim // 2, dtype=jnp.float32)
    inverse = jnp.exp(steps_up * (-2.0 * math.log(rope_base) / head_dim))
    return positions.astype(jnp.float32)[..., None] * inverse


def rotate(values, angles):
    half_dim = values.shape[-1] // 2
    cosine = jnp.cos(angles)
    sine_part = jnp.sin(angles)
    leading = values[..., :half_dim]
    trailing = values[..., half_dim:]
    return jnp.concatenate(
        [leading * cosine - trailing * sine_part, trailing * cosine + leading * sine_part], axis=-1
    )


def scale_rows(tokens, row_sums, gain_row, full_width):
    factor = lax.rsqrt(row_sums / full_width + norm_eps)
    return (tokens * factor[:, None] * gain_row.astype(jnp.float32)).astype(jnp.bfloat16)


def shards(
    embeds,
    lengths,
    k_cache,
    v_cache,
    gain_attn,
    gain_ffn,
    w_query,
    w_key,
    w_value,
    w_out,
    w_gate,
    w_up,
    w_down,
):
    local_rolls = embeds.shape[1]
    half_width = embeds.shape[2]
    full_width = half_width * lax.axis_size("narrow")
    kv_local = k_cache.shape[1]
    cache_len = k_cache.shape[2]
    group_size = HQ // KVH
    heads_local = kv_local * group_size
    query_cols = w_query.shape[1]
    key_cols = w_key.shape[1]
    ffn_cols = w_gate.shape[1]
    score_scale = 1.0 / math.sqrt(HD)
    cache_live = jnp.arange(cache_len, dtype=jnp.int32)[None, :] < lengths[:, None]
    tokens = embeds.reshape(STEPS * local_rolls, half_width).astype(jnp.float32)
    attn_sums = lax.psum(jnp.sum(tokens * tokens, axis=1), "narrow")
    normed = scale_rows(tokens, attn_sums, gain_attn, full_width)
    rows_all = lax.all_gather(normed, "wide", axis=0, tiled=True)
    partial = jnp.concatenate(
        [
            jnp.dot(rows_all, w_query, preferred_element_type=jnp.float32),
            jnp.dot(rows_all, w_key, preferred_element_type=jnp.float32),
            jnp.dot(rows_all, w_value, preferred_element_type=jnp.float32),
        ],
        axis=1,
    )
    full = lax.all_to_all(partial, "wide", split_axis=0, concat_axis=1, tiled=True)
    own = lax.psum_scatter(full, "narrow", scatter_dimension=1, tiled=True)
    own = own.reshape(STEPS, local_rolls, -1, query_cols + 2 * key_cols)
    query_own = own[..., :query_cols].reshape(STEPS, local_rolls, heads_local, HD)
    key_own = own[..., query_cols : query_cols + key_cols].reshape(STEPS, local_rolls, kv_local, HD)
    value_own = own[..., query_cols + key_cols :].reshape(STEPS, local_rolls, kv_local, HD)
    step_ids = jnp.arange(STEPS, dtype=jnp.int32)
    angles = angles_for(lengths[None, :] + step_ids[:, None], HD)[:, :, None, :]
    queries = rotate(query_own, angles).astype(jnp.bfloat16)
    keys_now = rotate(key_own, angles).astype(jnp.bfloat16)
    values_now = value_own.astype(jnp.bfloat16)
    keys_now = jnp.transpose(keys_now, (1, 2, 0, 3))
    values_now = jnp.transpose(values_now, (1, 2, 0, 3))
    grouped = queries.reshape(STEPS, local_rolls, kv_local, group_size, HD)
    grouped = jnp.transpose(grouped, (1, 2, 0, 3, 4)).reshape(
        local_rolls, kv_local, STEPS * group_size, HD
    )
    old_scores = (
        jnp.einsum("rkqd,rkcd->rkqc", grouped, k_cache, preferred_element_type=jnp.float32)
        * score_scale
    )
    old_scores = jnp.where(cache_live[:, None, None, :], old_scores, -jnp.inf)
    new_scores = (
        jnp.einsum("rkqd,rktd->rkqt", grouped, keys_now, preferred_element_type=jnp.float32)
        * score_scale
    )
    query_step = jnp.arange(STEPS * group_size, dtype=jnp.int32) // group_size
    new_live = step_ids[None, :] <= query_step[:, None]
    new_scores = jnp.where(new_live[None, None], new_scores, -jnp.inf)
    largest = jnp.maximum(
        jnp.max(old_scores, axis=-1, keepdims=True), jnp.max(new_scores, axis=-1, keepdims=True)
    )
    old_weights = jnp.exp(old_scores - largest)
    new_weights = jnp.exp(new_scores - largest)
    total = jnp.sum(old_weights, axis=-1, keepdims=True) + jnp.sum(
        new_weights, axis=-1, keepdims=True
    )
    mixed_heads = jnp.einsum(
        "rkqc,rkcd->rkqd",
        (old_weights / total).astype(jnp.bfloat16),
        v_cache,
        preferred_element_type=jnp.float32,
    ) + jnp.einsum(
        "rkqt,rktd->rkqd",
        (new_weights / total).astype(jnp.bfloat16),
        values_now,
        preferred_element_type=jnp.float32,
    )
    mixed_heads = mixed_heads.astype(jnp.bfloat16).reshape(
        local_rolls, kv_local, STEPS, group_size, HD
    )
    mixed_heads = jnp.transpose(mixed_heads, (2, 0, 1, 3, 4)).reshape(
        STEPS * local_rolls, heads_local * HD
    )
    out_part = jnp.dot(
        lax.all_gather(mixed_heads, "wide", axis=0, tiled=True),
        w_out,
        preferred_element_type=jnp.float32,
    )
    out_full = lax.all_to_all(
        out_part.astype(jnp.bfloat16), "wide", split_axis=0, concat_axis=1, tiled=True
    )
    out_own = lax.psum_scatter(out_full, "narrow", scatter_dimension=1, tiled=True).astype(
        jnp.float32
    )
    residual = tokens + out_own
    ffn_sums = lax.psum(jnp.sum(residual * residual, axis=1), "narrow")
    normed_ffn = scale_rows(residual, ffn_sums, gain_ffn, full_width)
    block_rows = lax.all_gather(normed_ffn, "wide", axis=0, tiled=True)
    lifted = jnp.concatenate(
        [
            jnp.dot(block_rows, w_gate, preferred_element_type=jnp.float32),
            jnp.dot(block_rows, w_up, preferred_element_type=jnp.float32),
        ],
        axis=1,
    )
    lifted_total = lax.psum(lifted.astype(jnp.bfloat16), "narrow").astype(jnp.float32)
    hidden = (jax.nn.silu(lifted_total[:, :ffn_cols]) * lifted_total[:, ffn_cols:]).astype(
        jnp.bfloat16
    )
    down_own = lax.psum_scatter(
        jnp.dot(hidden, w_down, preferred_element_type=jnp.float32).astype(jnp.bfloat16),
        "wide",
        scatter_dimension=0,
        tiled=True,
    ).astype(jnp.float32)
    result = (residual + down_own).reshape(STEPS, local_rolls, half_width)
    return (result, keys_now, values_now)


def solution(mesh):
    placed = (
        P(None, ("group", "wide"), "narrow"),
        P(("group", "wide")),
        P(("group", "wide"), "narrow", None, None),
        P(("group", "wide"), "narrow", None, None),
        P("narrow"),
        P("narrow"),
        P("narrow", "wide"),
        P("narrow", "wide"),
        P("narrow", "wide"),
        P("narrow", "wide"),
        P("narrow", "wide"),
        P("narrow", "wide"),
        P("wide", "narrow"),
    )
    return jax.shard_map(
        shards,
        mesh=mesh,
        in_specs=placed,
        out_specs=(
            P(None, ("group", "wide"), "narrow"),
            P(("group", "wide"), "narrow", None, None),
            P(("group", "wide"), "narrow", None, None),
        ),
        check_vma=False,
    )
```

```python
import math

import jax
import jax.numpy as jnp
from jax import lax
from jax.experimental import pallas as pl
from jax.experimental.pallas import tpu as pltpu
from jax.sharding import PartitionSpec as P

HQ = 40
KVH = 8
HD = 128
STEPS = 4


rope_base = 1000000.0
norm_eps = 1e-06


def angles_for(positions, head_dim):
    steps_up = jnp.arange(head_dim // 2, dtype=jnp.float32)
    inverse = jnp.exp(steps_up * (-2.0 * math.log(rope_base) / head_dim))
    return positions.astype(jnp.float32)[..., None] * inverse


def rotate(values, angles):
    half_dim = values.shape[-1] // 2
    cosine = jnp.cos(angles)
    sine_part = jnp.sin(angles)
    leading = values[..., :half_dim]
    trailing = values[..., half_dim:]
    return jnp.concatenate(
        [leading * cosine - trailing * sine_part, trailing * cosine + leading * sine_part], axis=-1
    )


def scale_rows(tokens, row_sums, gain_row, full_width):
    factor = lax.rsqrt(row_sums / full_width + norm_eps)
    return (tokens * factor[:, None] * gain_row.astype(jnp.float32)).astype(jnp.bfloat16)


def ring_place(device):
    row, side = device // 2, device % 2
    return row + side * (7 - 2 * row)


def ring_device(place):
    side = place // 4
    return 2 * (place + side * (7 - 2 * place)) + side


def greet_group():
    wide, narrow = lax.axis_index("wide"), lax.axis_index("narrow")
    barrier = pltpu.get_barrier_semaphore()
    for step in range(16):
        if step != 0:
            other_wide = (wide + step // 2) % 8
            other_narrow = (narrow + step % 2) % 2
            pl.semaphore_signal(
                barrier,
                inc=1,
                device_id={"wide": other_wide, "narrow": other_narrow},
                device_id_type=pl.DeviceIdType.MESH,
            )
    pl.semaphore_wait(barrier, 15)


def send(source, target, send_sem, recv_sem, wide, narrow):
    return pltpu.make_async_remote_copy(
        src_ref=source,
        dst_ref=target,
        send_sem=send_sem,
        recv_sem=recv_sem,
        device_id={"wide": wide, "narrow": narrow},
        device_id_type=pl.DeviceIdType.MESH,
    )


def ring_gather(blocks, send_sems, recv_sems):
    wide, narrow = lax.axis_index("wide"), lax.axis_index("narrow")
    place = ring_place(wide)
    right = ring_device((place + 1) % 8)
    left = ring_device((place + 7) % 8)
    half = blocks.shape[2] // 2
    ups, downs = [], []
    for hop in range(4):
        up_owner = ring_device((place + 8 - hop) % 8)
        down_owner = ring_device((place + hop) % 8)
        up_block, down_block = blocks.at[up_owner], blocks.at[down_owner]
        if hop == 3:
            up_block = blocks.at[up_owner, :, pl.ds(0, half)]
            down_block = blocks.at[down_owner, :, pl.ds(half, half)]
        if hop > 0:
            ups[-1].wait_recv()
        ups.append(
            send(up_block, up_block, send_sems.at[hop], recv_sems.at[hop], right, narrow)
        )
        ups[-1].start()
        if hop > 0:
            downs[-1].wait_recv()
        downs.append(
            send(down_block, down_block, send_sems.at[4 + hop], recv_sems.at[4 + hop], left, narrow)
        )
        downs[-1].start()
    ups[-1].wait_recv()
    downs[-1].wait_recv()
    for copy in ups + downs:
        copy.wait_send()


def norm_own(tokens, gain_ref, sums_out, sums_in, send_sem, recv_sem, full_width):
    wide, narrow = lax.axis_index("wide"), lax.axis_index("narrow")
    own_sums = jnp.sum(tokens * tokens, axis=1, keepdims=True)
    sums_out[...] = jnp.broadcast_to(own_sums, sums_out.shape)
    copy = send(sums_out, sums_in, send_sem, recv_sem, wide, 1 - narrow)
    copy.start()
    copy.wait()
    row_sums = own_sums + sums_in[:, 0:1]
    factor = lax.rsqrt(row_sums / full_width + norm_eps)
    return (tokens * factor * gain_ref[...].astype(jnp.float32)).astype(jnp.bfloat16)


def send_to_owners(parts, arrived, send_sems, recv_sems):
    wide, narrow = lax.axis_index("wide"), lax.axis_index("narrow")
    column_half = wide // 4
    my_slot = (wide % 4) * 2 + narrow
    keeps_own = column_half == narrow
    copies = []
    for step in range(8):
        owner = (wide + step) % 8
        copies.append(
            send(
                parts.at[owner],
                arrived.at[my_slot],
                send_sems.at[step],
                recv_sems.at[my_slot],
                owner,
                column_half,
            )
        )
    for copy in copies[1:]:
        copy.start()
    pl.when(jnp.logical_not(keeps_own))(copies[0].start)

    @pl.when(keeps_own)
    def _():
        arrived[my_slot] = parts[wide]

    for slot in range(8):
        comes = jnp.logical_or(wide != narrow * 4 + slot // 2, narrow != slot % 2)
        landed = send(
            parts.at[0],
            arrived.at[slot],
            send_sems.at[0],
            recv_sems.at[slot],
            wide,
            1 - narrow,
        )
        pl.when(comes)(landed.wait_recv)
    for copy in copies[1:]:
        copy.wait_send()
    pl.when(jnp.logical_not(keeps_own))(copies[0].wait_send)


def project_kernel(
    tokens_ref, gain_ref, w_query, w_key, w_value, own_ref,
    weights, blocks, parts, arrived, sums_out, sums_in,
    load_sems, ring_send, ring_recv, part_send, part_recv, sums_send, sums_recv,
):
    query_cols, key_cols = w_query.shape[1], w_key.shape[1]
    places = [(0, query_cols), (query_cols, key_cols), (query_cols + key_cols, key_cols)]
    loads = [
        pltpu.make_async_copy(matrix, weights.at[:, pl.ds(at, size)], load_sems.at[i])
        for i, (matrix, (at, size)) in enumerate(zip((w_query, w_key, w_value), places))
    ]
    for load in loads:
        load.start()
    greet_group()
    half_width = tokens_ref.shape[1]
    tokens = tokens_ref[...].astype(jnp.float32)
    normed = norm_own(
        tokens, gain_ref, sums_out, sums_in, sums_send.at[0], sums_recv.at[0], 2 * half_width
    )
    blocks[lax.axis_index("wide")] = normed
    ring_gather(blocks, ring_send, ring_recv)
    for load in loads:
        load.wait()
    rows = blocks[...].reshape(-1, half_width)
    sums = jnp.dot(rows, weights[...], preferred_element_type=jnp.float32)
    parts[...] = sums.reshape(parts.shape)
    send_to_owners(parts, arrived, part_send, part_recv)
    for peer in range(4):
        own_ref[peer] = arrived[2 * peer] + arrived[2 * peer + 1]


def finish_kernel(
    mixed_ref, tokens_ref, gain_ref, w_out, w_gate, w_up, w_down, result_ref,
    out_weights, gate_weights, up_weights, down_weights,
    mixed_blocks, out_parts, out_arrived, residual, normed_blocks, sums_out, sums_in,
    lifted, lifted_out, lifted_in, hidden, down_parts, down_arrived,
    load_sems, mixed_send, mixed_recv, part_send, part_recv, sums_send, sums_recv,
    normed_send, normed_recv, lifted_send, lifted_recv, down_send, down_recv,
):
    wide, narrow = lax.axis_index("wide"), lax.axis_index("narrow")
    half_width = tokens_ref.shape[1]
    loads = [
        pltpu.make_async_copy(matrix, place, load_sems.at[i])
        for i, (matrix, place) in enumerate(
            [(w_out, out_weights), (w_gate, gate_weights), (w_up, up_weights), (w_down, down_weights)]
        )
    ]
    for load in loads:
        load.start()
    greet_group()
    mixed_blocks[wide] = mixed_ref[...]
    ring_gather(mixed_blocks, mixed_send, mixed_recv)
    loads[0].wait()
    out_sums = jnp.dot(
        mixed_blocks[...].reshape(-1, half_width),
        out_weights[...],
        preferred_element_type=jnp.float32,
    )
    out_parts[...] = out_sums.astype(jnp.bfloat16).reshape(out_parts.shape)
    send_to_owners(out_parts, out_arrived, part_send, part_recv)
    out_cols = out_weights.shape[1]
    for peer in range(4):
        columns = pl.ds(peer * out_cols, out_cols)
        residual[:, columns] = (
            tokens_ref[:, columns].astype(jnp.float32)
            + out_arrived[2 * peer].astype(jnp.float32)
            + out_arrived[2 * peer + 1].astype(jnp.float32)
        )
    normed_blocks[wide] = norm_own(
        residual[...], gain_ref, sums_out, sums_in, sums_send.at[0], sums_recv.at[0], 2 * half_width
    )
    ring_gather(normed_blocks, normed_send, normed_recv)
    loads[1].wait()
    loads[2].wait()
    chunks, chunk = lifted.shape[0], lifted.shape[3]

    def lifted_copy(i):
        return send(
            lifted_out.at[i], lifted_in.at[i], lifted_send.at[i], lifted_recv.at[i], wide, 1 - narrow
        )

    def lift(i, carry):
        columns = pl.ds(pl.multiple_of(i * chunk, chunk), chunk)
        rows = normed_blocks[...].reshape(-1, half_width)
        for side, weights in enumerate((gate_weights, up_weights)):
            sums = jnp.dot(rows, weights[:, columns], preferred_element_type=jnp.float32)
            lifted[i, side] = sums
            lifted_out[i, side] = sums.astype(jnp.bfloat16)
        lifted_copy(i).start()
        return carry

    lax.fori_loop(0, chunks, lift, 0)

    def activate(i, carry):
        columns = pl.ds(pl.multiple_of(i * chunk, chunk), chunk)
        lifted_copy(i).wait()
        gate = lifted[i, 0] + lifted_in[i, 0].astype(jnp.float32)
        up = lifted[i, 1] + lifted_in[i, 1].astype(jnp.float32)
        hidden[:, columns] = (gate / (1.0 + jnp.exp(-gate)) * up).astype(jnp.bfloat16)
        return carry

    lax.fori_loop(0, chunks, activate, 0)
    loads[3].wait()
    down_chunk = 512

    def lower(i, carry):
        columns = pl.ds(pl.multiple_of(i * down_chunk, down_chunk), down_chunk)
        sums = jnp.dot(hidden[...], down_weights[:, columns], preferred_element_type=jnp.float32)
        down_parts[:, :, columns] = sums.astype(jnp.bfloat16).reshape(8, -1, down_chunk)
        return carry

    lax.fori_loop(0, half_width // down_chunk, lower, 0)
    copies = []
    for step in range(1, 8):
        owner = (wide + step) % 8
        copies.append(
            send(
                down_parts.at[owner],
                down_arrived.at[step - 1],
                down_send.at[step - 1],
                down_recv.at[step - 1],
                owner,
                narrow,
            )
        )
        copies[-1].start()
    total = residual[...] + down_parts[wide].astype(jnp.float32)
    for step, copy in enumerate(copies):
        copy.wait_recv()
        total = total + down_arrived[step].astype(jnp.float32)
    result_ref[...] = total
    for copy in copies:
        copy.wait_send()


def in_vmem():
    return pl.BlockSpec(memory_space=pltpu.VMEM)


def in_place():
    return pl.BlockSpec(memory_space=pl.ANY)


def project(tokens, gain, w_query, w_key, w_value):
    count, half_width = tokens.shape
    columns = w_query.shape[1] + 2 * w_key.shape[1]
    dma = pltpu.SemaphoreType.DMA
    return pl.pallas_call(
        project_kernel,
        out_shape=jax.ShapeDtypeStruct((4, count, columns), jnp.float32),
        in_specs=[in_vmem()] * 2 + [in_place()] * 3,
        out_specs=in_vmem(),
        scratch_shapes=[
            pltpu.VMEM((half_width, columns), jnp.bfloat16),
            pltpu.VMEM((8, count, half_width), jnp.bfloat16),
            pltpu.VMEM((8, count, columns), jnp.float32),
            pltpu.VMEM((8, count, columns), jnp.float32),
            pltpu.VMEM((count, 128), jnp.float32),
            pltpu.VMEM((count, 128), jnp.float32),
            dma((3,)), dma((8,)), dma((8,)), dma((8,)), dma((8,)), dma((1,)), dma((1,)),
        ],
        compiler_params=pltpu.CompilerParams(
            collective_id=0, has_side_effects=True, vmem_limit_bytes=32 * 2**20
        ),
        name="project",
    )(tokens, gain.reshape(1, -1), w_query, w_key, w_value)


def finish(mixed, tokens, gain, w_out, w_gate, w_up, w_down):
    count, half_width = tokens.shape
    out_cols, ffn_cols = w_out.shape[1], w_gate.shape[1]
    chunk = 256
    chunks = ffn_cols // chunk
    dma = pltpu.SemaphoreType.DMA
    return pl.pallas_call(
        finish_kernel,
        out_shape=jax.ShapeDtypeStruct((count, half_width), jnp.float32),
        in_specs=[in_vmem()] * 3 + [in_place()] * 4,
        out_specs=in_vmem(),
        scratch_shapes=[
            pltpu.VMEM(w_out.shape, jnp.bfloat16),
            pltpu.VMEM(w_gate.shape, jnp.bfloat16),
            pltpu.VMEM(w_up.shape, jnp.bfloat16),
            pltpu.VMEM(w_down.shape, jnp.bfloat16),
            pltpu.VMEM((8, count, half_width), jnp.bfloat16),
            pltpu.VMEM((8, count, out_cols), jnp.bfloat16),
            pltpu.VMEM((8, count, out_cols), jnp.bfloat16),
            pltpu.VMEM((count, half_width), jnp.float32),
            pltpu.VMEM((8, count, half_width), jnp.bfloat16),
            pltpu.VMEM((count, 128), jnp.float32),
            pltpu.VMEM((count, 128), jnp.float32),
            pltpu.VMEM((chunks, 2, 8 * count, chunk), jnp.float32),
            pltpu.VMEM((chunks, 2, 8 * count, chunk), jnp.bfloat16),
            pltpu.VMEM((chunks, 2, 8 * count, chunk), jnp.bfloat16),
            pltpu.VMEM((8 * count, ffn_cols), jnp.bfloat16),
            pltpu.VMEM((8, count, half_width), jnp.bfloat16),
            pltpu.VMEM((7, count, half_width), jnp.bfloat16),
            dma((4,)), dma((8,)), dma((8,)), dma((8,)), dma((8,)), dma((1,)), dma((1,)),
            dma((8,)), dma((8,)), dma((chunks,)), dma((chunks,)), dma((7,)), dma((7,)),
        ],
        compiler_params=pltpu.CompilerParams(
            collective_id=1, has_side_effects=True, vmem_limit_bytes=56 * 2**20
        ),
        name="finish",
    )(mixed, tokens, gain.reshape(1, -1), w_out, w_gate, w_up, w_down)


def shards(
    embeds,
    lengths,
    k_cache,
    v_cache,
    gain_attn,
    gain_ffn,
    w_query,
    w_key,
    w_value,
    w_out,
    w_gate,
    w_up,
    w_down,
):
    local_rolls = embeds.shape[1]
    half_width = embeds.shape[2]
    full_width = half_width * lax.axis_size("narrow")
    kv_local = k_cache.shape[1]
    cache_len = k_cache.shape[2]
    group_size = HQ // KVH
    heads_local = kv_local * group_size
    query_cols = w_query.shape[1]
    key_cols = w_key.shape[1]
    ffn_cols = w_gate.shape[1]
    score_scale = 1.0 / math.sqrt(HD)
    cache_live = jnp.arange(cache_len, dtype=jnp.int32)[None, :] < lengths[:, None]
    own_rows = embeds.reshape(STEPS * local_rolls, half_width)
    tokens = own_rows.astype(jnp.float32)
    by_kernel = (
        lax.axis_size("wide") == 8 and query_cols % 128 == 0 and ffn_cols % 256 == 0
    )
    if by_kernel:
        own = project(own_rows, gain_attn, w_query, w_key, w_value)
        own = jnp.transpose(own, (1, 0, 2))
    else:
        attn_sums = lax.psum(jnp.sum(tokens * tokens, axis=1), "narrow")
        normed = scale_rows(tokens, attn_sums, gain_attn, full_width)
        rows_all = lax.all_gather(normed, "wide", axis=0, tiled=True)
        partial = jnp.concatenate(
            [
                jnp.dot(rows_all, w_query, preferred_element_type=jnp.float32),
                jnp.dot(rows_all, w_key, preferred_element_type=jnp.float32),
                jnp.dot(rows_all, w_value, preferred_element_type=jnp.float32),
            ],
            axis=1,
        )
        full = lax.all_to_all(partial, "wide", split_axis=0, concat_axis=1, tiled=True)
        own = lax.psum_scatter(full, "narrow", scatter_dimension=1, tiled=True)
    own = own.reshape(STEPS, local_rolls, -1, query_cols + 2 * key_cols)
    query_own = own[..., :query_cols].reshape(STEPS, local_rolls, heads_local, HD)
    key_own = own[..., query_cols : query_cols + key_cols].reshape(STEPS, local_rolls, kv_local, HD)
    value_own = own[..., query_cols + key_cols :].reshape(STEPS, local_rolls, kv_local, HD)
    step_ids = jnp.arange(STEPS, dtype=jnp.int32)
    angles = angles_for(lengths[None, :] + step_ids[:, None], HD)[:, :, None, :]
    queries = rotate(query_own, angles).astype(jnp.bfloat16)
    keys_now = rotate(key_own, angles).astype(jnp.bfloat16)
    values_now = value_own.astype(jnp.bfloat16)
    keys_now = jnp.transpose(keys_now, (1, 2, 0, 3))
    values_now = jnp.transpose(values_now, (1, 2, 0, 3))
    grouped = queries.reshape(STEPS, local_rolls, kv_local, group_size, HD)
    grouped = jnp.transpose(grouped, (1, 2, 0, 3, 4)).reshape(
        local_rolls, kv_local, STEPS * group_size, HD
    )
    old_scores = (
        jnp.einsum("rkqd,rkcd->rkqc", grouped, k_cache, preferred_element_type=jnp.float32)
        * score_scale
    )
    old_scores = jnp.where(cache_live[:, None, None, :], old_scores, -jnp.inf)
    new_scores = (
        jnp.einsum("rkqd,rktd->rkqt", grouped, keys_now, preferred_element_type=jnp.float32)
        * score_scale
    )
    query_step = jnp.arange(STEPS * group_size, dtype=jnp.int32) // group_size
    new_live = step_ids[None, :] <= query_step[:, None]
    new_scores = jnp.where(new_live[None, None], new_scores, -jnp.inf)
    largest = jnp.maximum(
        jnp.max(old_scores, axis=-1, keepdims=True), jnp.max(new_scores, axis=-1, keepdims=True)
    )
    old_weights = jnp.exp(old_scores - largest)
    new_weights = jnp.exp(new_scores - largest)
    total = jnp.sum(old_weights, axis=-1, keepdims=True) + jnp.sum(
        new_weights, axis=-1, keepdims=True
    )
    mixed_heads = jnp.einsum(
        "rkqc,rkcd->rkqd",
        (old_weights / total).astype(jnp.bfloat16),
        v_cache,
        preferred_element_type=jnp.float32,
    ) + jnp.einsum(
        "rkqt,rktd->rkqd",
        (new_weights / total).astype(jnp.bfloat16),
        values_now,
        preferred_element_type=jnp.float32,
    )
    mixed_heads = mixed_heads.astype(jnp.bfloat16).reshape(
        local_rolls, kv_local, STEPS, group_size, HD
    )
    mixed_heads = jnp.transpose(mixed_heads, (2, 0, 1, 3, 4)).reshape(
        STEPS * local_rolls, heads_local * HD
    )
    if by_kernel:
        result = finish(mixed_heads, own_rows, gain_ffn, w_out, w_gate, w_up, w_down)
        return (result.reshape(STEPS, local_rolls, half_width), keys_now, values_now)
    out_part = jnp.dot(
        lax.all_gather(mixed_heads, "wide", axis=0, tiled=True),
        w_out,
        preferred_element_type=jnp.float32,
    )
    out_full = lax.all_to_all(
        out_part.astype(jnp.bfloat16), "wide", split_axis=0, concat_axis=1, tiled=True
    )
    out_own = lax.psum_scatter(out_full, "narrow", scatter_dimension=1, tiled=True).astype(
        jnp.float32
    )
    residual = tokens + out_own
    ffn_sums = lax.psum(jnp.sum(residual * residual, axis=1), "narrow")
    normed_ffn = scale_rows(residual, ffn_sums, gain_ffn, full_width)
    block_rows = lax.all_gather(normed_ffn, "wide", axis=0, tiled=True)
    lifted = jnp.concatenate(
        [
            jnp.dot(block_rows, w_gate, preferred_element_type=jnp.float32),
            jnp.dot(block_rows, w_up, preferred_element_type=jnp.float32),
        ],
        axis=1,
    )
    lifted_total = lax.psum(lifted.astype(jnp.bfloat16), "narrow").astype(jnp.float32)
    hidden = (jax.nn.silu(lifted_total[:, :ffn_cols]) * lifted_total[:, ffn_cols:]).astype(
        jnp.bfloat16
    )
    down_own = lax.psum_scatter(
        jnp.dot(hidden, w_down, preferred_element_type=jnp.float32).astype(jnp.bfloat16),
        "wide",
        scatter_dimension=0,
        tiled=True,
    ).astype(jnp.float32)
    result = (residual + down_own).reshape(STEPS, local_rolls, half_width)
    return (result, keys_now, values_now)


def solution(mesh):
    placed = (
        P(None, ("group", "wide"), "narrow"),
        P(("group", "wide")),
        P(("group", "wide"), "narrow", None, None),
        P(("group", "wide"), "narrow", None, None),
        P("narrow"),
        P("narrow"),
        P("narrow", "wide"),
        P("narrow", "wide"),
        P("narrow", "wide"),
        P("narrow", "wide"),
        P("narrow", "wide"),
        P("narrow", "wide"),
        P("wide", "narrow"),
    )
    return jax.shard_map(
        shards,
        mesh=mesh,
        in_specs=placed,
        out_specs=(
            P(None, ("group", "wide"), "narrow"),
            P(("group", "wide"), "narrow", None, None),
            P(("group", "wide"), "narrow", None, None),
        ),
        check_vma=False,
    )
```

```python
import math

import jax
import jax.numpy as jnp
from jax import lax
from jax.experimental import pallas as pl
from jax.experimental.pallas import tpu as pltpu
from jax.sharding import PartitionSpec as P

HQ = 40
KVH = 8
HD = 128
STEPS = 4


rope_base = 1000000.0
norm_eps = 1e-06


def angles_for(positions, head_dim):
    steps_up = jnp.arange(head_dim // 2, dtype=jnp.float32)
    inverse = jnp.exp(steps_up * (-2.0 * math.log(rope_base) / head_dim))
    return positions.astype(jnp.float32)[..., None] * inverse


def rotate(values, angles):
    half_dim = values.shape[-1] // 2
    cosine = jnp.cos(angles)
    sine_part = jnp.sin(angles)
    leading = values[..., :half_dim]
    trailing = values[..., half_dim:]
    return jnp.concatenate(
        [leading * cosine - trailing * sine_part, trailing * cosine + leading * sine_part], axis=-1
    )


def scale_rows(tokens, row_sums, gain_row, full_width):
    factor = lax.rsqrt(row_sums / full_width + norm_eps)
    return (tokens * factor[:, None] * gain_row.astype(jnp.float32)).astype(jnp.bfloat16)


def ring_place(device):
    row, side = device // 2, device % 2
    return row + side * (7 - 2 * row)


def ring_device(place):
    side = place // 4
    return 2 * (place + side * (7 - 2 * place)) + side


def greet_group():
    wide, narrow = lax.axis_index("wide"), lax.axis_index("narrow")
    barrier = pltpu.get_barrier_semaphore()
    for step in range(16):
        if step != 0:
            other_wide = (wide + step // 2) % 8
            other_narrow = (narrow + step % 2) % 2
            pl.semaphore_signal(
                barrier,
                inc=1,
                device_id={"wide": other_wide, "narrow": other_narrow},
                device_id_type=pl.DeviceIdType.MESH,
            )
    pl.semaphore_wait(barrier, 15)


def send(source, target, send_sem, recv_sem, wide, narrow):
    return pltpu.make_async_remote_copy(
        src_ref=source,
        dst_ref=target,
        send_sem=send_sem,
        recv_sem=recv_sem,
        device_id={"wide": wide, "narrow": narrow},
        device_id_type=pl.DeviceIdType.MESH,
    )


def ring_gather(blocks, send_sems, recv_sems):
    wide, narrow = lax.axis_index("wide"), lax.axis_index("narrow")
    place = ring_place(wide)
    right = ring_device((place + 1) % 8)
    left = ring_device((place + 7) % 8)
    half = blocks.shape[2] // 2
    ups, downs = {}, {}
    for hop in range(4):
        up_owner = ring_device((place + 8 - hop) % 8)
        down_owner = ring_device((place + hop) % 8)
        for part in range(2):
            columns = pl.ds(part * half, half)
            at = hop * 2 + part
            if hop < 3 or part == 0:
                block = blocks.at[up_owner, :, columns]
                if hop > 0:
                    ups[hop - 1, part].wait_recv()
                ups[hop, part] = send(
                    block, block, send_sems.at[at], recv_sems.at[at], right, narrow
                )
                ups[hop, part].start()
            if hop < 3 or part == 1:
                block = blocks.at[down_owner, :, columns]
                if hop > 0:
                    downs[hop - 1, part].wait_recv()
                downs[hop, part] = send(
                    block, block, send_sems.at[8 + at], recv_sems.at[8 + at], left, narrow
                )
                downs[hop, part].start()
    for copy in (ups[2, 1], downs[2, 0], ups[3, 0], downs[3, 1]):
        copy.wait_recv()
    for copy in list(ups.values()) + list(downs.values()):
        copy.wait_send()


def fill_rows(rows, steps_ref):
    count = steps_ref.shape[1]
    for step in range(steps_ref.shape[0]):
        rows[pl.ds(step * count, count), :] = steps_ref[step].astype(jnp.float32)


def norm_own(tokens, gain_ref, sums_out, sums_in, send_sem, recv_sem, full_width):
    wide, narrow = lax.axis_index("wide"), lax.axis_index("narrow")
    own_sums = jnp.sum(tokens * tokens, axis=1, keepdims=True)
    sums_out[...] = jnp.broadcast_to(own_sums, sums_out.shape)
    copy = send(sums_out, sums_in, send_sem, recv_sem, wide, 1 - narrow)
    copy.start()
    copy.wait()
    row_sums = own_sums + sums_in[:, 0:1]
    factor = lax.rsqrt(row_sums / full_width + norm_eps)
    return (tokens * factor * gain_ref[...].astype(jnp.float32).reshape(1, -1)).astype(
        jnp.bfloat16
    )


def send_to_owners(parts, arrived, send_sems, recv_sems):
    wide, narrow = lax.axis_index("wide"), lax.axis_index("narrow")
    column_half = wide // 4
    my_slot = (wide % 4) * 2 + narrow
    keeps_own = column_half == narrow
    copies = []
    for step in range(8):
        owner = (wide + step) % 8
        copies.append(
            send(
                parts.at[owner],
                arrived.at[my_slot],
                send_sems.at[step],
                recv_sems.at[my_slot],
                owner,
                column_half,
            )
        )
    for copy in copies[1:]:
        copy.start()
    pl.when(jnp.logical_not(keeps_own))(copies[0].start)

    @pl.when(keeps_own)
    def _():
        arrived[my_slot] = parts[wide]

    for slot in range(8):
        comes = jnp.logical_or(wide != narrow * 4 + slot // 2, narrow != slot % 2)
        landed = send(
            parts.at[0],
            arrived.at[slot],
            send_sems.at[0],
            recv_sems.at[slot],
            wide,
            1 - narrow,
        )
        pl.when(comes)(landed.wait_recv)
    for copy in copies[1:]:
        copy.wait_send()
    pl.when(jnp.logical_not(keeps_own))(copies[0].wait_send)


def project_kernel(
    tokens_ref, gain_ref, w_query, w_key, w_value, own_ref,
    weights, token_rows, blocks, parts, arrived, sums_out, sums_in,
    load_sems, ring_send, ring_recv, part_send, part_recv, sums_send, sums_recv,
):
    query_cols, key_cols = w_query.shape[1], w_key.shape[1]
    places = [(0, query_cols), (query_cols, key_cols), (query_cols + key_cols, key_cols)]
    loads = [
        pltpu.make_async_copy(matrix, weights.at[:, pl.ds(at, size)], load_sems.at[i])
        for i, (matrix, (at, size)) in enumerate(zip((w_query, w_key, w_value), places))
    ]
    for load in loads:
        load.start()
    greet_group()
    half_width = tokens_ref.shape[2]
    fill_rows(token_rows, tokens_ref)
    normed = norm_own(
        token_rows[...], gain_ref, sums_out, sums_in, sums_send.at[0], sums_recv.at[0], 2 * half_width
    )
    blocks[lax.axis_index("wide")] = normed
    ring_gather(blocks, ring_send, ring_recv)
    for load in loads:
        load.wait()
    rows = blocks[...].reshape(-1, half_width)
    sums = jnp.dot(rows, weights[...], preferred_element_type=jnp.float32)
    parts[...] = sums.astype(jnp.bfloat16).reshape(parts.shape)
    send_to_owners(parts, arrived, part_send, part_recv)
    for peer in range(4):
        own_ref[peer] = arrived[2 * peer].astype(jnp.float32) + arrived[2 * peer + 1].astype(
            jnp.float32
        )


def finish_kernel(
    mixed_ref, tokens_ref, gain_ref, w_out, w_gate, w_up, w_down, result_ref,
    out_weights, gate_weights, up_weights, down_weights,
    mixed_blocks, out_parts, out_arrived, residual, normed_blocks, sums_out, sums_in,
    lifted, lifted_out, lifted_in, hidden, down_parts, side_arrived, pair_sums, row_arrived,
    load_sems, mixed_send, mixed_recv, part_send, part_recv, sums_send, sums_recv,
    normed_send, normed_recv, lifted_send, lifted_recv, side_send, side_recv,
    row_send, row_recv,
):
    wide, narrow = lax.axis_index("wide"), lax.axis_index("narrow")
    half_width = tokens_ref.shape[2]
    loads = [
        pltpu.make_async_copy(matrix, place, load_sems.at[i])
        for i, (matrix, place) in enumerate(
            [(w_out, out_weights), (w_gate, gate_weights), (w_up, up_weights), (w_down, down_weights)]
        )
    ]
    for load in loads:
        load.start()
    greet_group()
    fill_rows(residual, tokens_ref)
    mixed_blocks[wide] = mixed_ref[...]
    ring_gather(mixed_blocks, mixed_send, mixed_recv)
    loads[0].wait()
    out_sums = jnp.dot(
        mixed_blocks[...].reshape(-1, half_width),
        out_weights[...],
        preferred_element_type=jnp.float32,
    )
    out_parts[...] = out_sums.astype(jnp.bfloat16).reshape(out_parts.shape)
    send_to_owners(out_parts, out_arrived, part_send, part_recv)
    out_cols = out_weights.shape[1]
    for peer in range(4):
        columns = pl.ds(peer * out_cols, out_cols)
        residual[:, columns] = (
            residual[:, columns]
            + out_arrived[2 * peer].astype(jnp.float32)
            + out_arrived[2 * peer + 1].astype(jnp.float32)
        )
    normed_blocks[wide] = norm_own(
        residual[...], gain_ref, sums_out, sums_in, sums_send.at[0], sums_recv.at[0], 2 * half_width
    )
    ring_gather(normed_blocks, normed_send, normed_recv)
    loads[1].wait()
    loads[2].wait()
    chunks, chunk = lifted.shape[0], lifted.shape[3]

    def lifted_copy(i):
        return send(
            lifted_out.at[i], lifted_in.at[i], lifted_send.at[i], lifted_recv.at[i], wide, 1 - narrow
        )

    def lift(i, carry):
        columns = pl.ds(pl.multiple_of(i * chunk, chunk), chunk)
        rows = normed_blocks[...].reshape(-1, half_width)
        for side, weights in enumerate((gate_weights, up_weights)):
            sums = jnp.dot(rows, weights[:, columns], preferred_element_type=jnp.float32)
            lifted[i, side] = sums
            lifted_out[i, side] = sums.astype(jnp.bfloat16)
        lifted_copy(i).start()
        return carry

    lax.fori_loop(0, chunks, lift, 0)

    def activate(i, carry):
        columns = pl.ds(pl.multiple_of(i * chunk, chunk), chunk)
        lifted_copy(i).wait()
        gate = lifted[i, 0] + lifted_in[i, 0].astype(jnp.float32)
        up = lifted[i, 1] + lifted_in[i, 1].astype(jnp.float32)
        hidden[:, columns] = (gate / (1.0 + jnp.exp(-gate)) * up).astype(jnp.bfloat16)
        return carry

    lax.fori_loop(0, chunks, activate, 0)
    loads[3].wait()
    row, side = wide // 2, wide % 2
    down_chunk = 512
    chunk_count = half_width // down_chunk
    side_copies, row_copies = [], []

    def add_side(i):
        columns = pl.ds(i * down_chunk, down_chunk)
        side_copies[i].wait_recv()
        pair_sums[:, :, columns] = (
            down_parts[side, :, :, columns].astype(jnp.float32)
            + side_arrived[:, :, columns].astype(jnp.float32)
        ).astype(jnp.bfloat16)
        for step in range(1, 4):
            at = i * 3 + step - 1
            other = (row + step) % 4
            row_copies.append(
                send(
                    pair_sums.at[other, :, columns],
                    row_arrived.at[step - 1, :, columns],
                    row_send.at[at],
                    row_recv.at[at],
                    2 * other + side,
                    narrow,
                )
            )
            row_copies[-1].start()

    for i in range(chunk_count):
        columns = pl.ds(i * down_chunk, down_chunk)
        sums = jnp.dot(hidden[...], down_weights[:, columns], preferred_element_type=jnp.float32)
        sums = sums.astype(jnp.bfloat16).reshape(4, 2, -1, down_chunk)
        down_parts[0, :, :, columns] = sums[:, 0]
        down_parts[1, :, :, columns] = sums[:, 1]
        side_copies.append(
            send(
                down_parts.at[1 - side, :, :, columns],
                side_arrived.at[:, :, columns],
                side_send.at[i],
                side_recv.at[i],
                2 * row + 1 - side,
                narrow,
            )
        )
        side_copies[-1].start()
        if i > 0:
            add_side(i - 1)
    add_side(chunk_count - 1)
    count = result_ref.shape[1]
    for i in range(chunk_count):
        columns = pl.ds(i * down_chunk, down_chunk)
        total = residual[:, columns] + pair_sums[row, :, columns].astype(jnp.float32)
        for step in range(3):
            row_copies[i * 3 + step].wait_recv()
            total = total + row_arrived[step, :, columns].astype(jnp.float32)
        for step in range(result_ref.shape[0]):
            result_ref[step, :, columns] = total[step * count : (step + 1) * count]
    for copy in side_copies + row_copies:
        copy.wait_send()


def in_vmem():
    return pl.BlockSpec(memory_space=pltpu.VMEM)


def in_place():
    return pl.BlockSpec(memory_space=pl.ANY)


def project(tokens, gain, w_query, w_key, w_value):
    count, half_width = tokens.shape[0] * tokens.shape[1], tokens.shape[2]
    columns = w_query.shape[1] + 2 * w_key.shape[1]
    dma = pltpu.SemaphoreType.DMA
    return pl.pallas_call(
        project_kernel,
        out_shape=jax.ShapeDtypeStruct((4, count, columns), jnp.float32),
        in_specs=[in_vmem()] * 2 + [in_place()] * 3,
        out_specs=in_vmem(),
        scratch_shapes=[
            pltpu.VMEM((half_width, columns), jnp.bfloat16),
            pltpu.VMEM((count, half_width), jnp.float32),
            pltpu.VMEM((8, count, half_width), jnp.bfloat16),
            pltpu.VMEM((8, count, columns), jnp.bfloat16),
            pltpu.VMEM((8, count, columns), jnp.bfloat16),
            pltpu.VMEM((count, 128), jnp.float32),
            pltpu.VMEM((count, 128), jnp.float32),
            dma((3,)), dma((16,)), dma((16,)), dma((8,)), dma((8,)), dma((1,)), dma((1,)),
        ],
        compiler_params=pltpu.CompilerParams(
            collective_id=0, has_side_effects=True, vmem_limit_bytes=56 * 2**20
        ),
        name="project",
    )(tokens, gain, w_query, w_key, w_value)


def finish(mixed, tokens, gain, w_out, w_gate, w_up, w_down):
    count, half_width = tokens.shape[0] * tokens.shape[1], tokens.shape[2]
    out_cols, ffn_cols = w_out.shape[1], w_gate.shape[1]
    chunk = 256
    chunks = ffn_cols // chunk
    dma = pltpu.SemaphoreType.DMA
    return pl.pallas_call(
        finish_kernel,
        out_shape=jax.ShapeDtypeStruct(tokens.shape, jnp.float32),
        in_specs=[in_vmem()] * 3 + [in_place()] * 4,
        out_specs=in_vmem(),
        scratch_shapes=[
            pltpu.VMEM(w_out.shape, jnp.bfloat16),
            pltpu.VMEM(w_gate.shape, jnp.bfloat16),
            pltpu.VMEM(w_up.shape, jnp.bfloat16),
            pltpu.VMEM(w_down.shape, jnp.bfloat16),
            pltpu.VMEM((8, count, half_width), jnp.bfloat16),
            pltpu.VMEM((8, count, out_cols), jnp.bfloat16),
            pltpu.VMEM((8, count, out_cols), jnp.bfloat16),
            pltpu.VMEM((count, half_width), jnp.float32),
            pltpu.VMEM((8, count, half_width), jnp.bfloat16),
            pltpu.VMEM((count, 128), jnp.float32),
            pltpu.VMEM((count, 128), jnp.float32),
            pltpu.VMEM((chunks, 2, 8 * count, chunk), jnp.float32),
            pltpu.VMEM((chunks, 2, 8 * count, chunk), jnp.bfloat16),
            pltpu.VMEM((chunks, 2, 8 * count, chunk), jnp.bfloat16),
            pltpu.VMEM((8 * count, ffn_cols), jnp.bfloat16),
            pltpu.VMEM((2, 4, count, half_width), jnp.bfloat16),
            pltpu.VMEM((4, count, half_width), jnp.bfloat16),
            pltpu.VMEM((4, count, half_width), jnp.bfloat16),
            pltpu.VMEM((3, count, half_width), jnp.bfloat16),
            dma((4,)), dma((16,)), dma((16,)), dma((8,)), dma((8,)), dma((1,)), dma((1,)),
            dma((16,)), dma((16,)), dma((chunks,)), dma((chunks,)),
            dma((half_width // 512,)), dma((half_width // 512,)),
            dma((3 * (half_width // 512),)), dma((3 * (half_width // 512),)),
        ],
        compiler_params=pltpu.CompilerParams(
            collective_id=1, has_side_effects=True, vmem_limit_bytes=56 * 2**20
        ),
        name="finish",
    )(mixed, tokens, gain, w_out, w_gate, w_up, w_down)


def shards(
    embeds,
    lengths,
    k_cache,
    v_cache,
    gain_attn,
    gain_ffn,
    w_query,
    w_key,
    w_value,
    w_out,
    w_gate,
    w_up,
    w_down,
):
    local_rolls = embeds.shape[1]
    half_width = embeds.shape[2]
    full_width = half_width * lax.axis_size("narrow")
    kv_local = k_cache.shape[1]
    cache_len = k_cache.shape[2]
    group_size = HQ // KVH
    heads_local = kv_local * group_size
    query_cols = w_query.shape[1]
    key_cols = w_key.shape[1]
    ffn_cols = w_gate.shape[1]
    score_scale = 1.0 / math.sqrt(HD)
    cache_live = jnp.arange(cache_len, dtype=jnp.int32)[None, :] < lengths[:, None]
    own_rows = embeds.reshape(STEPS * local_rolls, half_width)
    tokens = own_rows.astype(jnp.float32)
    by_kernel = (
        lax.axis_size("wide") == 8 and query_cols % 128 == 0 and ffn_cols % 256 == 0
    )
    if by_kernel:
        own = project(embeds, gain_attn, w_query, w_key, w_value)
        own = jnp.transpose(own, (1, 0, 2))
    else:
        attn_sums = lax.psum(jnp.sum(tokens * tokens, axis=1), "narrow")
        normed = scale_rows(tokens, attn_sums, gain_attn, full_width)
        rows_all = lax.all_gather(normed, "wide", axis=0, tiled=True)
        partial = jnp.concatenate(
            [
                jnp.dot(rows_all, w_query, preferred_element_type=jnp.float32),
                jnp.dot(rows_all, w_key, preferred_element_type=jnp.float32),
                jnp.dot(rows_all, w_value, preferred_element_type=jnp.float32),
            ],
            axis=1,
        )
        full = lax.all_to_all(partial, "wide", split_axis=0, concat_axis=1, tiled=True)
        own = lax.psum_scatter(full, "narrow", scatter_dimension=1, tiled=True)
    own = own.reshape(STEPS, local_rolls, -1, query_cols + 2 * key_cols)
    query_own = own[..., :query_cols].reshape(STEPS, local_rolls, heads_local, HD)
    key_own = own[..., query_cols : query_cols + key_cols].reshape(STEPS, local_rolls, kv_local, HD)
    value_own = own[..., query_cols + key_cols :].reshape(STEPS, local_rolls, kv_local, HD)
    step_ids = jnp.arange(STEPS, dtype=jnp.int32)
    angles = angles_for(lengths[None, :] + step_ids[:, None], HD)[:, :, None, :]
    queries = rotate(query_own, angles).astype(jnp.bfloat16)
    keys_now = rotate(key_own, angles).astype(jnp.bfloat16)
    values_now = value_own.astype(jnp.bfloat16)
    keys_now = jnp.transpose(keys_now, (1, 2, 0, 3))
    values_now = jnp.transpose(values_now, (1, 2, 0, 3))
    grouped = queries.reshape(STEPS, local_rolls, kv_local, group_size, HD)
    grouped = jnp.transpose(grouped, (1, 2, 0, 3, 4)).reshape(
        local_rolls, kv_local, STEPS * group_size, HD
    )
    old_scores = (
        jnp.einsum("rkqd,rkcd->rkqc", grouped, k_cache, preferred_element_type=jnp.float32)
        * score_scale
    )
    old_scores = jnp.where(cache_live[:, None, None, :], old_scores, -jnp.inf)
    new_scores = (
        jnp.einsum("rkqd,rktd->rkqt", grouped, keys_now, preferred_element_type=jnp.float32)
        * score_scale
    )
    query_step = jnp.arange(STEPS * group_size, dtype=jnp.int32) // group_size
    new_live = step_ids[None, :] <= query_step[:, None]
    new_scores = jnp.where(new_live[None, None], new_scores, -jnp.inf)
    largest = jnp.maximum(
        jnp.max(old_scores, axis=-1, keepdims=True), jnp.max(new_scores, axis=-1, keepdims=True)
    )
    old_weights = jnp.exp(old_scores - largest)
    new_weights = jnp.exp(new_scores - largest)
    total = jnp.sum(old_weights, axis=-1, keepdims=True) + jnp.sum(
        new_weights, axis=-1, keepdims=True
    )
    mixed_heads = jnp.einsum(
        "rkqc,rkcd->rkqd",
        (old_weights / total).astype(jnp.bfloat16),
        v_cache,
        preferred_element_type=jnp.float32,
    ) + jnp.einsum(
        "rkqt,rktd->rkqd",
        (new_weights / total).astype(jnp.bfloat16),
        values_now,
        preferred_element_type=jnp.float32,
    )
    mixed_heads = mixed_heads.astype(jnp.bfloat16).reshape(
        local_rolls, kv_local, STEPS, group_size, HD
    )
    mixed_heads = jnp.transpose(mixed_heads, (2, 0, 1, 3, 4)).reshape(
        STEPS * local_rolls, heads_local * HD
    )
    if by_kernel:
        result = finish(mixed_heads, embeds, gain_ffn, w_out, w_gate, w_up, w_down)
        return (result, keys_now, values_now)
    out_part = jnp.dot(
        lax.all_gather(mixed_heads, "wide", axis=0, tiled=True),
        w_out,
        preferred_element_type=jnp.float32,
    )
    out_full = lax.all_to_all(
        out_part.astype(jnp.bfloat16), "wide", split_axis=0, concat_axis=1, tiled=True
    )
    out_own = lax.psum_scatter(out_full, "narrow", scatter_dimension=1, tiled=True).astype(
        jnp.float32
    )
    residual = tokens + out_own
    ffn_sums = lax.psum(jnp.sum(residual * residual, axis=1), "narrow")
    normed_ffn = scale_rows(residual, ffn_sums, gain_ffn, full_width)
    block_rows = lax.all_gather(normed_ffn, "wide", axis=0, tiled=True)
    lifted = jnp.concatenate(
        [
            jnp.dot(block_rows, w_gate, preferred_element_type=jnp.float32),
            jnp.dot(block_rows, w_up, preferred_element_type=jnp.float32),
        ],
        axis=1,
    )
    lifted_total = lax.psum(lifted.astype(jnp.bfloat16), "narrow").astype(jnp.float32)
    hidden = (jax.nn.silu(lifted_total[:, :ffn_cols]) * lifted_total[:, ffn_cols:]).astype(
        jnp.bfloat16
    )
    down_own = lax.psum_scatter(
        jnp.dot(hidden, w_down, preferred_element_type=jnp.float32).astype(jnp.bfloat16),
        "wide",
        scatter_dimension=0,
        tiled=True,
    ).astype(jnp.float32)
    result = (residual + down_own).reshape(STEPS, local_rolls, half_width)
    return (result, keys_now, values_now)


def solution(mesh):
    placed = (
        P(None, ("group", "wide"), "narrow"),
        P(("group", "wide")),
        P(("group", "wide"), "narrow", None, None),
        P(("group", "wide"), "narrow", None, None),
        P("narrow"),
        P("narrow"),
        P("narrow", "wide"),
        P("narrow", "wide"),
        P("narrow", "wide"),
        P("narrow", "wide"),
        P("narrow", "wide"),
        P("narrow", "wide"),
        P("wide", "narrow"),
    )
    return jax.shard_map(
        shards,
        mesh=mesh,
        in_specs=placed,
        out_specs=(
            P(None, ("group", "wide"), "narrow"),
            P(("group", "wide"), "narrow", None, None),
            P(("group", "wide"), "narrow", None, None),
        ),
        check_vma=False,
    )
```

```python
import math

import jax
import jax.numpy as jnp
from jax import lax
from jax.experimental import pallas as pl
from jax.experimental.pallas import tpu as pltpu
from jax.sharding import PartitionSpec as P

HQ = 40
KVH = 8
HD = 128
STEPS = 4


rope_base = 1000000.0
norm_eps = 1e-06


def angles_for(positions, head_dim):
    steps_up = jnp.arange(head_dim // 2, dtype=jnp.float32)
    inverse = jnp.exp(steps_up * (-2.0 * math.log(rope_base) / head_dim))
    return positions.astype(jnp.float32)[..., None] * inverse


def rotate(values, angles):
    half_dim = values.shape[-1] // 2
    cosine = jnp.cos(angles)
    sine_part = jnp.sin(angles)
    leading = values[..., :half_dim]
    trailing = values[..., half_dim:]
    return jnp.concatenate(
        [leading * cosine - trailing * sine_part, trailing * cosine + leading * sine_part], axis=-1
    )


def scale_rows(tokens, row_sums, gain_row, full_width):
    factor = lax.rsqrt(row_sums / full_width + norm_eps)
    return (tokens * factor[:, None] * gain_row.astype(jnp.float32)).astype(jnp.bfloat16)


def greet_group():
    wide, narrow = lax.axis_index("wide"), lax.axis_index("narrow")
    barrier = pltpu.get_barrier_semaphore()
    for step in range(16):
        if step != 0:
            other_wide = (wide + step // 2) % 8
            other_narrow = (narrow + step % 2) % 2
            pl.semaphore_signal(
                barrier,
                inc=1,
                device_id={"wide": other_wide, "narrow": other_narrow},
                device_id_type=pl.DeviceIdType.MESH,
            )
    pl.semaphore_wait(barrier, 15)


def send(source, target, send_sem, recv_sem, wide, narrow):
    return pltpu.make_async_remote_copy(
        src_ref=source,
        dst_ref=target,
        send_sem=send_sem,
        recv_sem=recv_sem,
        device_id={"wide": wide, "narrow": narrow},
        device_id_type=pl.DeviceIdType.MESH,
    )


def gather_blocks(blocks, send_sems, recv_sems):
    wide, narrow = lax.axis_index("wide"), lax.axis_index("narrow")
    row, side = wide // 2, wide % 2
    beside = 2 * row + 1 - side
    half = blocks.shape[2] // 2

    def share(owner, part, at, target):
        block = blocks.at[owner, :, pl.ds(part * half, half)]
        at = part * 8 + at
        return send(block, block, send_sems.at[at], recv_sems.at[at], target, narrow)

    along, across = {}, []
    for part in range(2):
        for step in range(1, 4):
            along[part, step] = share(wide, part, step, 2 * ((row + step) % 4) + side)
            along[part, step].start()
        across.append(share(wide, part, 0, beside))
        across[-1].start()
    for part in range(2):
        for step in range(1, 4):
            along[part, step].wait_recv()
            across.append(share(2 * ((row + 4 - step) % 4) + side, part, 3 + step, beside))
            across[-1].start()
    for copy in across:
        copy.wait_recv()
    for copy in list(along.values()) + across:
        copy.wait_send()


def fill_rows(rows, steps_ref):
    count = steps_ref.shape[1]
    for step in range(steps_ref.shape[0]):
        rows[pl.ds(step * count, count), :] = steps_ref[step].astype(jnp.float32)


def norm_own(tokens, gain_ref, sums_out, sums_in, send_sem, recv_sem, full_width):
    wide, narrow = lax.axis_index("wide"), lax.axis_index("narrow")
    own_sums = jnp.sum(tokens * tokens, axis=1, keepdims=True)
    sums_out[...] = jnp.broadcast_to(own_sums, sums_out.shape)
    copy = send(sums_out, sums_in, send_sem, recv_sem, wide, 1 - narrow)
    copy.start()
    copy.wait()
    row_sums = own_sums + sums_in[:, 0:1]
    factor = lax.rsqrt(row_sums / full_width + norm_eps)
    return (tokens * factor * gain_ref[...].astype(jnp.float32).reshape(1, -1)).astype(
        jnp.bfloat16
    )


def send_to_owners(parts, arrived, send_sems, recv_sems):
    wide, narrow = lax.axis_index("wide"), lax.axis_index("narrow")
    column_half = wide // 4
    my_slot = (wide % 4) * 2 + narrow
    keeps_own = column_half == narrow
    copies = []
    for step in range(8):
        owner = (wide + step) % 8
        copies.append(
            send(
                parts.at[owner],
                arrived.at[my_slot],
                send_sems.at[step],
                recv_sems.at[my_slot],
                owner,
                column_half,
            )
        )
    for copy in copies[1:]:
        copy.start()
    pl.when(jnp.logical_not(keeps_own))(copies[0].start)

    @pl.when(keeps_own)
    def _():
        arrived[my_slot] = parts[wide]

    for slot in range(8):
        comes = jnp.logical_or(wide != narrow * 4 + slot // 2, narrow != slot % 2)
        landed = send(
            parts.at[0],
            arrived.at[slot],
            send_sems.at[0],
            recv_sems.at[slot],
            wide,
            1 - narrow,
        )
        pl.when(comes)(landed.wait_recv)
    for copy in copies[1:]:
        copy.wait_send()
    pl.when(jnp.logical_not(keeps_own))(copies[0].wait_send)


def project_kernel(
    tokens_ref, gain_ref, w_query, w_key, w_value, own_ref,
    weights, token_rows, blocks, parts, arrived, sums_out, sums_in,
    load_sems, ring_send, ring_recv, part_send, part_recv, sums_send, sums_recv,
):
    query_cols, key_cols = w_query.shape[1], w_key.shape[1]
    places = [(0, query_cols), (query_cols, key_cols), (query_cols + key_cols, key_cols)]
    loads = [
        pltpu.make_async_copy(matrix, weights.at[:, pl.ds(at, size)], load_sems.at[i])
        for i, (matrix, (at, size)) in enumerate(zip((w_query, w_key, w_value), places))
    ]
    for load in loads:
        load.start()
    greet_group()
    half_width = tokens_ref.shape[2]
    fill_rows(token_rows, tokens_ref)
    normed = norm_own(
        token_rows[...], gain_ref, sums_out, sums_in, sums_send.at[0], sums_recv.at[0], 2 * half_width
    )
    blocks[lax.axis_index("wide")] = normed
    gather_blocks(blocks, ring_send, ring_recv)
    for load in loads:
        load.wait()
    rows = blocks[...].reshape(-1, half_width)
    sums = jnp.dot(rows, weights[...], preferred_element_type=jnp.float32)
    parts[...] = sums.astype(jnp.bfloat16).reshape(parts.shape)
    send_to_owners(parts, arrived, part_send, part_recv)
    for peer in range(4):
        own_ref[peer] = arrived[2 * peer].astype(jnp.float32) + arrived[2 * peer + 1].astype(
            jnp.float32
        )


def finish_kernel(
    mixed_ref, tokens_ref, gain_ref, w_out, w_gate, w_up, w_down, result_ref,
    out_weights, gate_weights, up_weights, down_weights,
    mixed_blocks, out_parts, out_arrived, residual, normed_blocks, sums_out, sums_in,
    lifted, lifted_out, lifted_in, hidden, down_parts, side_arrived, pair_sums, row_arrived,
    load_sems, mixed_send, mixed_recv, part_send, part_recv, sums_send, sums_recv,
    normed_send, normed_recv, lifted_send, lifted_recv, side_send, side_recv,
    row_send, row_recv,
):
    wide, narrow = lax.axis_index("wide"), lax.axis_index("narrow")
    half_width = tokens_ref.shape[2]
    loads = [
        pltpu.make_async_copy(matrix, place, load_sems.at[i])
        for i, (matrix, place) in enumerate(
            [(w_out, out_weights), (w_gate, gate_weights), (w_up, up_weights), (w_down, down_weights)]
        )
    ]
    for load in loads:
        load.start()
    greet_group()
    fill_rows(residual, tokens_ref)
    mixed_blocks[wide] = mixed_ref[...]
    gather_blocks(mixed_blocks, mixed_send, mixed_recv)
    loads[0].wait()
    out_sums = jnp.dot(
        mixed_blocks[...].reshape(-1, half_width),
        out_weights[...],
        preferred_element_type=jnp.float32,
    )
    out_parts[...] = out_sums.astype(jnp.bfloat16).reshape(out_parts.shape)
    send_to_owners(out_parts, out_arrived, part_send, part_recv)
    out_cols = out_weights.shape[1]
    for peer in range(4):
        columns = pl.ds(peer * out_cols, out_cols)
        residual[:, columns] = (
            residual[:, columns]
            + out_arrived[2 * peer].astype(jnp.float32)
            + out_arrived[2 * peer + 1].astype(jnp.float32)
        )
    normed_blocks[wide] = norm_own(
        residual[...], gain_ref, sums_out, sums_in, sums_send.at[0], sums_recv.at[0], 2 * half_width
    )
    gather_blocks(normed_blocks, normed_send, normed_recv)
    loads[1].wait()
    loads[2].wait()
    chunks, chunk = lifted.shape[0], lifted.shape[3]

    def lifted_copy(i):
        return send(
            lifted_out.at[i], lifted_in.at[i], lifted_send.at[i], lifted_recv.at[i], wide, 1 - narrow
        )

    def lift(i, carry):
        columns = pl.ds(pl.multiple_of(i * chunk, chunk), chunk)
        rows = normed_blocks[...].reshape(-1, half_width)
        for side, weights in enumerate((gate_weights, up_weights)):
            sums = jnp.dot(rows, weights[:, columns], preferred_element_type=jnp.float32)
            lifted[i, side] = sums
            lifted_out[i, side] = sums.astype(jnp.bfloat16)
        lifted_copy(i).start()
        return carry

    lax.fori_loop(0, chunks, lift, 0)

    def activate(i, carry):
        columns = pl.ds(pl.multiple_of(i * chunk, chunk), chunk)
        lifted_copy(i).wait()
        gate = lifted[i, 0] + lifted_in[i, 0].astype(jnp.float32)
        up = lifted[i, 1] + lifted_in[i, 1].astype(jnp.float32)
        hidden[:, columns] = (gate / (1.0 + jnp.exp(-gate)) * up).astype(jnp.bfloat16)
        return carry

    lax.fori_loop(0, chunks, activate, 0)
    loads[3].wait()
    row, side = wide // 2, wide % 2
    down_chunk = 512
    chunk_count = half_width // down_chunk
    side_copies, row_copies = [], []

    def add_side(i):
        columns = pl.ds(i * down_chunk, down_chunk)
        side_copies[i].wait_recv()
        pair_sums[:, :, columns] = (
            down_parts[side, :, :, columns].astype(jnp.float32)
            + side_arrived[:, :, columns].astype(jnp.float32)
        ).astype(jnp.bfloat16)
        for step in range(1, 4):
            at = i * 3 + step - 1
            other = (row + step) % 4
            row_copies.append(
                send(
                    pair_sums.at[other, :, columns],
                    row_arrived.at[step - 1, :, columns],
                    row_send.at[at],
                    row_recv.at[at],
                    2 * other + side,
                    narrow,
                )
            )
            row_copies[-1].start()

    for i in range(chunk_count):
        columns = pl.ds(i * down_chunk, down_chunk)
        sums = jnp.dot(hidden[...], down_weights[:, columns], preferred_element_type=jnp.float32)
        sums = sums.astype(jnp.bfloat16).reshape(4, 2, -1, down_chunk)
        down_parts[0, :, :, columns] = sums[:, 0]
        down_parts[1, :, :, columns] = sums[:, 1]
        side_copies.append(
            send(
                down_parts.at[1 - side, :, :, columns],
                side_arrived.at[:, :, columns],
                side_send.at[i],
                side_recv.at[i],
                2 * row + 1 - side,
                narrow,
            )
        )
        side_copies[-1].start()
        if i > 0:
            add_side(i - 1)
    add_side(chunk_count - 1)
    count = result_ref.shape[1]
    for i in range(chunk_count):
        columns = pl.ds(i * down_chunk, down_chunk)
        total = residual[:, columns] + pair_sums[row, :, columns].astype(jnp.float32)
        for step in range(3):
            row_copies[i * 3 + step].wait_recv()
            total = total + row_arrived[step, :, columns].astype(jnp.float32)
        for step in range(result_ref.shape[0]):
            result_ref[step, :, columns] = total[step * count : (step + 1) * count]
    for copy in side_copies + row_copies:
        copy.wait_send()


def in_vmem():
    return pl.BlockSpec(memory_space=pltpu.VMEM)


def in_place():
    return pl.BlockSpec(memory_space=pl.ANY)


def project(tokens, gain, w_query, w_key, w_value):
    count, half_width = tokens.shape[0] * tokens.shape[1], tokens.shape[2]
    columns = w_query.shape[1] + 2 * w_key.shape[1]
    dma = pltpu.SemaphoreType.DMA
    return pl.pallas_call(
        project_kernel,
        out_shape=jax.ShapeDtypeStruct((4, count, columns), jnp.float32),
        in_specs=[in_vmem()] * 2 + [in_place()] * 3,
        out_specs=in_vmem(),
        scratch_shapes=[
            pltpu.VMEM((half_width, columns), jnp.bfloat16),
            pltpu.VMEM((count, half_width), jnp.float32),
            pltpu.VMEM((8, count, half_width), jnp.bfloat16),
            pltpu.VMEM((8, count, columns), jnp.bfloat16),
            pltpu.VMEM((8, count, columns), jnp.bfloat16),
            pltpu.VMEM((count, 128), jnp.float32),
            pltpu.VMEM((count, 128), jnp.float32),
            dma((3,)), dma((16,)), dma((16,)), dma((8,)), dma((8,)), dma((1,)), dma((1,)),
        ],
        compiler_params=pltpu.CompilerParams(
            collective_id=0, has_side_effects=True, vmem_limit_bytes=56 * 2**20
        ),
        name="project",
    )(tokens, gain, w_query, w_key, w_value)


def finish(mixed, tokens, gain, w_out, w_gate, w_up, w_down):
    count, half_width = tokens.shape[0] * tokens.shape[1], tokens.shape[2]
    out_cols, ffn_cols = w_out.shape[1], w_gate.shape[1]
    chunk = 256
    chunks = ffn_cols // chunk
    dma = pltpu.SemaphoreType.DMA
    return pl.pallas_call(
        finish_kernel,
        out_shape=jax.ShapeDtypeStruct(tokens.shape, jnp.float32),
        in_specs=[in_vmem()] * 3 + [in_place()] * 4,
        out_specs=in_vmem(),
        scratch_shapes=[
            pltpu.VMEM(w_out.shape, jnp.bfloat16),
            pltpu.VMEM(w_gate.shape, jnp.bfloat16),
            pltpu.VMEM(w_up.shape, jnp.bfloat16),
            pltpu.VMEM(w_down.shape, jnp.bfloat16),
            pltpu.VMEM((8, count, half_width), jnp.bfloat16),
            pltpu.VMEM((8, count, out_cols), jnp.bfloat16),
            pltpu.VMEM((8, count, out_cols), jnp.bfloat16),
            pltpu.VMEM((count, half_width), jnp.float32),
            pltpu.VMEM((8, count, half_width), jnp.bfloat16),
            pltpu.VMEM((count, 128), jnp.float32),
            pltpu.VMEM((count, 128), jnp.float32),
            pltpu.VMEM((chunks, 2, 8 * count, chunk), jnp.float32),
            pltpu.VMEM((chunks, 2, 8 * count, chunk), jnp.bfloat16),
            pltpu.VMEM((chunks, 2, 8 * count, chunk), jnp.bfloat16),
            pltpu.VMEM((8 * count, ffn_cols), jnp.bfloat16),
            pltpu.VMEM((2, 4, count, half_width), jnp.bfloat16),
            pltpu.VMEM((4, count, half_width), jnp.bfloat16),
            pltpu.VMEM((4, count, half_width), jnp.bfloat16),
            pltpu.VMEM((3, count, half_width), jnp.bfloat16),
            dma((4,)), dma((16,)), dma((16,)), dma((8,)), dma((8,)), dma((1,)), dma((1,)),
            dma((16,)), dma((16,)), dma((chunks,)), dma((chunks,)),
            dma((half_width // 512,)), dma((half_width // 512,)),
            dma((3 * (half_width // 512),)), dma((3 * (half_width // 512),)),
        ],
        compiler_params=pltpu.CompilerParams(
            collective_id=1, has_side_effects=True, vmem_limit_bytes=56 * 2**20
        ),
        name="finish",
    )(mixed, tokens, gain, w_out, w_gate, w_up, w_down)


def shards(
    embeds,
    lengths,
    k_cache,
    v_cache,
    gain_attn,
    gain_ffn,
    w_query,
    w_key,
    w_value,
    w_out,
    w_gate,
    w_up,
    w_down,
):
    local_rolls = embeds.shape[1]
    half_width = embeds.shape[2]
    full_width = half_width * lax.axis_size("narrow")
    kv_local = k_cache.shape[1]
    cache_len = k_cache.shape[2]
    group_size = HQ // KVH
    heads_local = kv_local * group_size
    query_cols = w_query.shape[1]
    key_cols = w_key.shape[1]
    ffn_cols = w_gate.shape[1]
    score_scale = 1.0 / math.sqrt(HD)
    cache_live = jnp.arange(cache_len, dtype=jnp.int32)[None, :] < lengths[:, None]
    own_rows = embeds.reshape(STEPS * local_rolls, half_width)
    tokens = own_rows.astype(jnp.float32)
    by_kernel = (
        lax.axis_size("wide") == 8 and query_cols % 128 == 0 and ffn_cols % 256 == 0
    )
    if by_kernel:
        own = project(embeds, gain_attn, w_query, w_key, w_value)
        own = jnp.transpose(own, (1, 0, 2))
    else:
        attn_sums = lax.psum(jnp.sum(tokens * tokens, axis=1), "narrow")
        normed = scale_rows(tokens, attn_sums, gain_attn, full_width)
        rows_all = lax.all_gather(normed, "wide", axis=0, tiled=True)
        partial = jnp.concatenate(
            [
                jnp.dot(rows_all, w_query, preferred_element_type=jnp.float32),
                jnp.dot(rows_all, w_key, preferred_element_type=jnp.float32),
                jnp.dot(rows_all, w_value, preferred_element_type=jnp.float32),
            ],
            axis=1,
        )
        full = lax.all_to_all(partial, "wide", split_axis=0, concat_axis=1, tiled=True)
        own = lax.psum_scatter(full, "narrow", scatter_dimension=1, tiled=True)
    own = own.reshape(STEPS, local_rolls, -1, query_cols + 2 * key_cols)
    query_own = own[..., :query_cols].reshape(STEPS, local_rolls, heads_local, HD)
    key_own = own[..., query_cols : query_cols + key_cols].reshape(STEPS, local_rolls, kv_local, HD)
    value_own = own[..., query_cols + key_cols :].reshape(STEPS, local_rolls, kv_local, HD)
    step_ids = jnp.arange(STEPS, dtype=jnp.int32)
    angles = angles_for(lengths[None, :] + step_ids[:, None], HD)[:, :, None, :]
    queries = rotate(query_own, angles).astype(jnp.bfloat16)
    keys_now = rotate(key_own, angles).astype(jnp.bfloat16)
    values_now = value_own.astype(jnp.bfloat16)
    keys_now = jnp.transpose(keys_now, (1, 2, 0, 3))
    values_now = jnp.transpose(values_now, (1, 2, 0, 3))
    grouped = queries.reshape(STEPS, local_rolls, kv_local, group_size, HD)
    grouped = jnp.transpose(grouped, (1, 2, 0, 3, 4)).reshape(
        local_rolls, kv_local, STEPS * group_size, HD
    )
    old_scores = (
        jnp.einsum("rkqd,rkcd->rkqc", grouped, k_cache, preferred_element_type=jnp.float32)
        * score_scale
    )
    old_scores = jnp.where(cache_live[:, None, None, :], old_scores, -jnp.inf)
    new_scores = (
        jnp.einsum("rkqd,rktd->rkqt", grouped, keys_now, preferred_element_type=jnp.float32)
        * score_scale
    )
    query_step = jnp.arange(STEPS * group_size, dtype=jnp.int32) // group_size
    new_live = step_ids[None, :] <= query_step[:, None]
    new_scores = jnp.where(new_live[None, None], new_scores, -jnp.inf)
    largest = jnp.maximum(
        jnp.max(old_scores, axis=-1, keepdims=True), jnp.max(new_scores, axis=-1, keepdims=True)
    )
    old_weights = jnp.exp(old_scores - largest)
    new_weights = jnp.exp(new_scores - largest)
    total = jnp.sum(old_weights, axis=-1, keepdims=True) + jnp.sum(
        new_weights, axis=-1, keepdims=True
    )
    mixed_heads = jnp.einsum(
        "rkqc,rkcd->rkqd",
        (old_weights / total).astype(jnp.bfloat16),
        v_cache,
        preferred_element_type=jnp.float32,
    ) + jnp.einsum(
        "rkqt,rktd->rkqd",
        (new_weights / total).astype(jnp.bfloat16),
        values_now,
        preferred_element_type=jnp.float32,
    )
    mixed_heads = mixed_heads.astype(jnp.bfloat16).reshape(
        local_rolls, kv_local, STEPS, group_size, HD
    )
    mixed_heads = jnp.transpose(mixed_heads, (2, 0, 1, 3, 4)).reshape(
        STEPS * local_rolls, heads_local * HD
    )
    if by_kernel:
        result = finish(mixed_heads, embeds, gain_ffn, w_out, w_gate, w_up, w_down)
        return (result, keys_now, values_now)
    out_part = jnp.dot(
        lax.all_gather(mixed_heads, "wide", axis=0, tiled=True),
        w_out,
        preferred_element_type=jnp.float32,
    )
    out_full = lax.all_to_all(
        out_part.astype(jnp.bfloat16), "wide", split_axis=0, concat_axis=1, tiled=True
    )
    out_own = lax.psum_scatter(out_full, "narrow", scatter_dimension=1, tiled=True).astype(
        jnp.float32
    )
    residual = tokens + out_own
    ffn_sums = lax.psum(jnp.sum(residual * residual, axis=1), "narrow")
    normed_ffn = scale_rows(residual, ffn_sums, gain_ffn, full_width)
    block_rows = lax.all_gather(normed_ffn, "wide", axis=0, tiled=True)
    lifted = jnp.concatenate(
        [
            jnp.dot(block_rows, w_gate, preferred_element_type=jnp.float32),
            jnp.dot(block_rows, w_up, preferred_element_type=jnp.float32),
        ],
        axis=1,
    )
    lifted_total = lax.psum(lifted.astype(jnp.bfloat16), "narrow").astype(jnp.float32)
    hidden = (jax.nn.silu(lifted_total[:, :ffn_cols]) * lifted_total[:, ffn_cols:]).astype(
        jnp.bfloat16
    )
    down_own = lax.psum_scatter(
        jnp.dot(hidden, w_down, preferred_element_type=jnp.float32).astype(jnp.bfloat16),
        "wide",
        scatter_dimension=0,
        tiled=True,
    ).astype(jnp.float32)
    result = (residual + down_own).reshape(STEPS, local_rolls, half_width)
    return (result, keys_now, values_now)


def solution(mesh):
    placed = (
        P(None, ("group", "wide"), "narrow"),
        P(("group", "wide")),
        P(("group", "wide"), "narrow", None, None),
        P(("group", "wide"), "narrow", None, None),
        P("narrow"),
        P("narrow"),
        P("narrow", "wide"),
        P("narrow", "wide"),
        P("narrow", "wide"),
        P("narrow", "wide"),
        P("narrow", "wide"),
        P("narrow", "wide"),
        P("wide", "narrow"),
    )
    return jax.shard_map(
        shards,
        mesh=mesh,
        in_specs=placed,
        out_specs=(
            P(None, ("group", "wide"), "narrow"),
            P(("group", "wide"), "narrow", None, None),
            P(("group", "wide"), "narrow", None, None),
        ),
        check_vma=False,
    )
```
